256 devices in a mesh: band: 16 (over z, x_hi), cuts: 16 (over x_lo, y, core).
Axes of the slice: x: 4 (x_hi: 2, x_lo: 2; x = x_hi * 2 + x_lo), y: 4, z: 8, core: 2. Of those that a mesh axis runs over, the one named last changes fastest.
Arguments:
- var_feat: bfloat16 [1310720, 128], P(('band', 'cuts')), may hold values from -6 to 6
- con_feat: bfloat16 [32768, 128], P(('band', 'cuts')), may hold values from -6 to 6
- slot_column_block: int32 [40960], P(('band', 'cuts')), may hold values from 0 to 39
- slot_constraint_block: int32 [40960], P(('band', 'cuts')), may hold values from 0 to 31
- block_count: int32 [256], P(('band', 'cuts')), may hold values from 40 to 160, as said below
- incidence_coefficients: int32 [40960, 128, 128], P(('band', 'cuts')), may hold values from -3 to 4
- con_first: bfloat16 [256, 256], replicated, may hold values from -0.375 to 0.375
- con_bias: float32 [256], replicated, may hold values from -3 to 3
- con_second: bfloat16 [256, 256], replicated, may hold values from -0.375 to 0.375
- con_third: bfloat16 [256, 128], replicated, may hold values from -0.375 to 0.375
- con_gain: float32 [128], replicated, may hold values from 0.1 to 1.9
- con_shift: float32 [128], replicated, may hold values from -3 to 3
- var_first: bfloat16 [256, 256], replicated, may hold values from -0.375 to 0.375
- var_bias: float32 [256], replicated, may hold values from -3 to 3
- var_second: bfloat16 [256, 256], replicated, may hold values from -0.375 to 0.375
- var_third: bfloat16 [256, 128], replicated, may hold values from -0.375 to 0.375
- var_gain: float32 [128], replicated, may hold values from 0.1 to 1.9
- var_shift: float32 [128], replicated, may hold values from -3 to 3
Outputs:
- con_new: bfloat16 [32768, 128], P(('band', 'cuts'))
- var_new: bfloat16 [1310720, 128], P(('band', 'cuts'))
The draws below stay inside these ranges and needn't reach their ends.
Inputs may be any that keep to these rules, and one draw needn't show every extreme that they name: Each device's live slots are its first block_count slots; in every draw one eighth of the devices hold 160 live slots and some device holds 40.
All inputs are finite; a program needn't handle non-finite values.
Results may differ from the reference program's by a relative error of at most 0.0075.
Values may be sent and summed in bfloat16 or wider, within the bound.
No kernel may reach another device: no remote copies, remote signals or barrier semaphores. Data moves between devices by JAX's collectives and lax.ppermute only.
A program may use at most 128 MiB of HBM per device.

```python
import math
import jax
import jax.numpy as jnp
from jax import lax

W = 128
HID = 256
INCIDENCE_ORDER = 128
CONSTRAINT_BLKS = 1
PATTERN_BLOCKS = 40
NB = 160
NV = 1310720
NC = 32768
TOTAL_SLOTS = 40960
N_BAND = 16
N_CUTS = 16


def draw_block_count(key, part):
    device_total = N_BAND * N_CUTS
    first_key, second_key = jax.random.split(key)
    live_slots = PATTERN_BLOCKS + jax.random.randint(first_key, (device_total,), 0, PATTERN_BLOCKS + 1)
    shuffled = jax.random.permutation(second_key, device_total)
    full_rank = jnp.zeros((device_total,), jnp.int32).at[shuffled].set(jnp.arange(device_total, dtype=jnp.int32))
    heavy = full_rank < device_total // 8
    live_slots = jnp.where(heavy, 4 * PATTERN_BLOCKS, live_slots)
    live_slots = jnp.where(full_rank == device_total - 1, PATTERN_BLOCKS, live_slots)
    return live_slots.astype(jnp.int32)


def plant(result, key, least, top_value):
    shape = result.shape
    spot = [jax.random.randint(jax.random.fold_in(key, axis), (), 0, shape[axis]) for axis in range(len(shape))]
    result = result.at[tuple(spot)].set(least)
    longest = shape.index(max(shape))
    spot[longest] = (spot[longest] + 1) % shape[longest]
    return result.at[tuple(spot)].set(top_value)


def levels(rng, extent, cuts, low, largest):
    level = 1.0
    for axis_at, parts in cuts:
        heights = jax.random.uniform(jax.random.fold_in(jax.random.fold_in(rng, 6), axis_at), (parts,), jnp.float32, low / len(cuts), largest / len(cuts))
        level = level * jnp.repeat(jnp.exp(heights), extent[axis_at] // parts).reshape((-1,) + (1,) * (len(extent) - 1 - axis_at))
    return level


def scatter_about(rng, extent, scale, bound, shards=(), kind=jnp.bfloat16):
    entries = scale * jax.random.normal(rng, extent, jnp.float32)
    if shards:
        entries = entries * levels(rng, extent, shards, -0.22, 0.18)
    return jnp.clip(entries, -bound, bound).astype(kind)


def setup_inputs(seed: int = 0) -> dict:
    seeds = jax.random.split(jax.random.key(seed), 19)
    var_feat = scatter_about(seeds[0], (NV, W), 1.0, 6.0, ((0, 256),))
    con_feat = scatter_about(seeds[1], (NC, W), 1.0, 6.0, ((0, 256),))
    slot_column_block = plant(jax.random.randint(seeds[2], (TOTAL_SLOTS,), 0, PATTERN_BLOCKS), jax.random.fold_in(seeds[2], 1), 0, PATTERN_BLOCKS - 1).astype(jnp.int32)
    slot_constraint_block = plant(jax.random.randint(seeds[3], (TOTAL_SLOTS,), 0, 2 * CONSTRAINT_BLKS * N_CUTS), jax.random.fold_in(seeds[3], 1), 0, (2 * CONSTRAINT_BLKS * N_CUTS) - 1).astype(jnp.int32)
    block_count = draw_block_count(jax.random.fold_in(seeds[18], 71), 0)
    incidence_coefficients = plant(jax.random.randint(seeds[5], (TOTAL_SLOTS, INCIDENCE_ORDER, INCIDENCE_ORDER), -3, 5), jax.random.fold_in(seeds[5], 1), -3, 4).astype(jnp.int32)
    con_first = scatter_about(seeds[6], (2 * W, HID), (2 * W) ** -0.5, 0.375)
    con_bias = scatter_about(seeds[7], (HID,), 0.5, 3.0, (), jnp.float32)
    con_second = scatter_about(seeds[8], (HID, HID), HID ** -0.5, 0.375)
    con_third = scatter_about(seeds[9], (HID, W), HID ** -0.5, 0.375)
    con_gain = jnp.clip(1.0 + 0.18 * jax.random.normal(seeds[10], (W,), jnp.float32), 0.1, 1.9)
    con_shift = scatter_about(seeds[11], (W,), 0.5, 3.0, (), jnp.float32)
    var_first = scatter_about(seeds[12], (2 * W, HID), (2 * W) ** -0.5, 0.375)
    var_bias = scatter_about(seeds[13], (HID,), 0.5, 3.0, (), jnp.float32)
    var_second = scatter_about(seeds[14], (HID, HID), HID ** -0.5, 0.375)
    var_third = scatter_about(seeds[15], (HID, W), HID ** -0.5, 0.375)
    var_gain = jnp.clip(1.0 + 0.18 * jax.random.normal(seeds[16], (W,), jnp.float32), 0.1, 1.9)
    var_shift = scatter_about(seeds[17], (W,), 0.5, 3.0, (), jnp.float32)
    return {"var_feat": var_feat, "con_feat": con_feat, "slot_column_block": slot_column_block, "slot_constraint_block": slot_constraint_block, "block_count": block_count, "incidence_coefficients": incidence_coefficients, "con_first": con_first, "con_bias": con_bias, "con_second": con_second, "con_third": con_third, "con_gain": con_gain, "con_shift": con_shift, "var_first": var_first, "var_bias": var_bias, "var_second": var_second, "var_third": var_third, "var_gain": var_gain, "var_shift": var_shift}


EPS = 1e-05

def layer_norm(values, gain, offset):
    center = values - lax.optimization_barrier(jnp.mean(values, axis=-1, keepdims=True))
    spread = lax.optimization_barrier(jnp.mean(center * center, axis=-1, keepdims=True))
    return center * lax.rsqrt(spread + EPS) * gain + offset

def node_update(feats, scaled_agg, w_first, bias, w_second, w_third, gain, offset):
    joined = jnp.concatenate([feats, scaled_agg.astype(jnp.bfloat16)], axis=1)
    hidden = jnp.maximum(jnp.dot(joined, w_first, preferred_element_type=jnp.float32) + bias, 0.0).astype(jnp.bfloat16)
    middle = jnp.maximum(jnp.dot(hidden, w_second, preferred_element_type=jnp.float32), 0.0).astype(jnp.bfloat16)
    output = jnp.dot(middle, w_third, preferred_element_type=jnp.float32)
    return layer_norm(feats.astype(jnp.float32) + output, gain, offset).astype(jnp.bfloat16)

def reference(var_feat, con_feat, slot_column_block, slot_constraint_block, block_count, incidence_coefficients, con_first, con_bias, con_second, con_third, con_gain, con_shift, var_first, var_bias, var_second, var_third, var_gain, var_shift):
    device_total = N_BAND * N_CUTS
    band_blocks = CONSTRAINT_BLKS * N_CUTS
    band_rows = band_blocks * INCIDENCE_ORDER
    width = var_feat.shape[1]
    var_blocks = var_feat.reshape(device_total, PATTERN_BLOCKS, INCIDENCE_ORDER, width)
    col_index = slot_column_block.reshape(device_total, NB)
    row_index = slot_constraint_block.reshape(device_total, NB)
    coef_all = incidence_coefficients.reshape(device_total, NB, INCIDENCE_ORDER, INCIDENCE_ORDER)
    slot_ids = jnp.arange(NB, dtype=jnp.int32)
    row_ids = jnp.arange(2 * band_blocks, dtype=jnp.int32)
    col_ids = jnp.arange(PATTERN_BLOCKS, dtype=jnp.int32)
    highest = lax.Precision.HIGHEST

    def accumulate(carry, device):
        live = (slot_ids < block_count[device]).astype(jnp.float32)
        picked = jnp.take(var_blocks[device], col_index[device], axis=0).astype(jnp.float32)
        coef = coef_all[device].astype(jnp.float32)
        products = jnp.einsum('sij,sjw->siw', coef, picked, precision=highest)
        selector = (row_index[device][None, :] == row_ids[:, None]).astype(jnp.float32) * live[None, :]
        term = jnp.einsum('rs,siw->riw', selector, products, precision=highest).reshape(2 * band_rows, width)
        start = device // N_CUTS * band_rows
        current = lax.dynamic_slice_in_dim(carry, start, 2 * band_rows, 0)
        return (lax.dynamic_update_slice_in_dim(carry, current + term, start, 0), None)
    padded = jnp.zeros((NC + band_rows, width), jnp.float32)
    con_agg, _ = lax.scan(accumulate, padded, jnp.arange(device_total, dtype=jnp.int32))
    con_agg = con_agg[:NC] * (1.0 / math.sqrt(INCIDENCE_ORDER * NB))
    con_new = node_update(con_feat, con_agg, con_first, con_bias, con_second, con_third, con_gain, con_shift)
    con_padded = jnp.concatenate([con_new, jnp.zeros((band_rows, width), jnp.bfloat16)], axis=0)

    def update(device):
        live = (slot_ids < block_count[device]).astype(jnp.float32)
        start = device // N_CUTS * band_rows
        window = lax.dynamic_slice_in_dim(con_padded, start, 2 * band_rows, 0).reshape(2 * band_blocks, INCIDENCE_ORDER, width)
        picked = jnp.take(window, row_index[device], axis=0).astype(jnp.float32)
        coef = coef_all[device].astype(jnp.float32)
        products = jnp.einsum('sij,siw->sjw', coef, picked, precision=highest)
        selector = (col_index[device][None, :] == col_ids[:, None]).astype(jnp.float32) * live[None, :]
        var_agg = jnp.einsum('cs,sjw->cjw', selector, products, precision=highest).reshape(PATTERN_BLOCKS * INCIDENCE_ORDER, width)
        var_agg = var_agg * (1.0 / math.sqrt(4 * INCIDENCE_ORDER))
        own_feat = var_blocks[device].reshape(PATTERN_BLOCKS * INCIDENCE_ORDER, width)
        return node_update(own_feat, var_agg, var_first, var_bias, var_second, var_third, var_gain, var_shift)
    var_new = lax.map(update, jnp.arange(device_total, dtype=jnp.int32)).reshape(NV, width)
    return (con_new, var_new)
```

```python
import functools
import math

import jax
import jax.numpy as jnp
from jax import lax
from jax.experimental import pallas as pl
from jax.experimental.pallas import tpu as pltpu
from jax.sharding import PartitionSpec as P

EPS = 1e-05
F32 = jnp.float32
BF16 = jnp.bfloat16
GROUP = 8
VMEM_BYTES = 40 * 1024 * 1024


def place(index):
    return index // 8, (index // 2) % 4, index % 2


def position(x, y, core):
    return x * 8 + y * 2 + core


def layer_norm(values, gain, offset):
    center = values - jnp.mean(values, axis=-1, keepdims=True)
    spread = jnp.mean(center * center, axis=-1, keepdims=True)
    return center * lax.rsqrt(spread + EPS) * gain + offset


def node_update(feats, scaled_agg, w_first, bias, w_second, w_third, gain, offset):
    joined = jnp.concatenate([feats, scaled_agg.astype(BF16)], axis=1)
    hidden = jnp.maximum(jnp.dot(joined, w_first, preferred_element_type=F32) + bias, 0.0).astype(BF16)
    middle = jnp.maximum(jnp.dot(hidden, w_second, preferred_element_type=F32), 0.0).astype(BF16)
    output = jnp.dot(middle, w_third, preferred_element_type=F32)
    return layer_norm(feats.astype(F32) + output, gain, offset).astype(BF16)


def coefficient_copy(coef_ref, coef_buf, sem, group):
    rows = pl.ds(group * GROUP, GROUP)
    return pltpu.make_async_copy(coef_ref.at[rows], coef_buf.at[rows], sem.at[group])


def start_coefficients(coef_ref, coef_buf, sem, groups):
    def start(group, carry):
        coefficient_copy(coef_ref, coef_buf, sem, group).start()
        return carry

    lax.fori_loop(0, groups, start, 0)


def clear(acc):
    def body(block, carry):
        acc[block] = jnp.zeros(acc.shape[1:], acc.dtype)
        return carry

    lax.fori_loop(0, acc.shape[0], body, 0)


def to_constraints_kernel(
    me_ref, count_ref, col_ref, row_ref, coef_ref, feat_ref, keep_ref, give_ref, coef_buf, feat_buf, acc, table, sem, feat_sem
):
    count = count_ref[0]
    groups = (count + GROUP - 1) // GROUP
    feat_copy = pltpu.make_async_copy(feat_ref, feat_buf, feat_sem)
    feat_copy.start()
    start_coefficients(coef_ref, coef_buf, sem, groups)
    my_x, my_y, my_core = place(me_ref[0])
    for q in range(32):
        x, y, core = place(q % 16)
        table[q] = (core ^ my_core) * 16 + ((y - my_y) & 3) * 4 + (x ^ my_x) * 2 + q // 16
    clear(acc)
    feat_copy.wait()

    def step(group, carry):
        coefficient_copy(coef_ref, coef_buf, sem, group).wait()
        for k in range(GROUP):
            slot = group * GROUP + k
            block = jnp.where(slot < count, table[row_ref[slot]], 32)
            product = jnp.dot(
                coef_buf[slot].astype(BF16), feat_buf[col_ref[slot]], preferred_element_type=F32
            )
            acc[block] += product
        return carry

    lax.fori_loop(0, groups, step, 0)
    keep_ref[...] = acc[pl.ds(0, 16)]
    give_ref[...] = acc[pl.ds(16, 16)].astype(BF16)


def constraint_kernel(
    kept, first, second, third, feat, w_first, bias, w_second, w_third, gain, offset, scale, out, out_t
):
    agg = kept[...] + first[...].astype(F32) + second[...].astype(F32) + third[...].astype(F32)
    new = node_update(
        feat[...], agg * scale, w_first[...], bias[...], w_second[...], w_third[...], gain[...], offset[...]
    )
    out[...] = new
    out_t[...] = new.astype(F32).T.astype(BF16)


def to_columns_kernel(
    pieces,
    scale,
    tile,
    me_ref,
    count_ref,
    col_ref,
    row_ref,
    coef_ref,
    feat_ref,
    *refs,
):
    piece_refs = refs[:pieces]
    w_first, bias, w_second, w_third, gain, offset = refs[pieces : pieces + 6]
    out_ref = refs[pieces + 6]
    coef_buf, feat_buf, window, acc, out_buf, table, sem, feat_sem, out_sem = refs[pieces + 7 :]
    count = count_ref[0]
    groups = (count + GROUP - 1) // GROUP
    start_coefficients(coef_ref, coef_buf, sem, groups)
    feat_copy = pltpu.make_async_copy(feat_ref, feat_buf, feat_sem)
    feat_copy.start()
    my_x, my_y, my_core = place(me_ref[0])
    for q in range(32):
        x, y, core = place(q % 16)
        table[q] = (core ^ my_core) * 16 + ((my_y - y) & 3) * 4 + (q // 16) * 2 + (x ^ my_x)
    base = 0
    for ref in piece_refs:
        window[pl.ds(base, ref.shape[0])] = ref[...]
        base += ref.shape[0]
    clear(acc)
    blocks = acc.shape[0] - 1

    def step(group, carry):
        coefficient_copy(coef_ref, coef_buf, sem, group).wait()
        for k in range(GROUP):
            slot = group * GROUP + k
            block = jnp.where(slot < count, col_ref[slot], blocks)
            product = jnp.dot(
                window[table[row_ref[slot]]], coef_buf[slot].astype(BF16), preferred_element_type=F32
            )
            acc[block] += product
        return carry

    lax.fori_loop(0, groups, step, 0)
    feat_copy.wait()

    def out_copy(at):
        rows = pl.ds(at * tile, tile)
        return pltpu.make_async_copy(out_buf.at[rows], out_ref.at[rows], out_sem.at[at])

    def update(at, carry):
        agg = jnp.concatenate([(acc[at * tile + k].T * scale) for k in range(tile)], axis=0)
        feats = feat_buf[pl.ds(at * tile, tile)].reshape(-1, agg.shape[1])
        new = node_update(
            feats, agg, w_first[...], bias[...], w_second[...], w_third[...], gain[...], offset[...]
        )
        out_buf[pl.ds(at * tile, tile)] = new.reshape(tile, -1, agg.shape[1])
        out_copy(at).start()
        return carry

    steps = blocks // tile
    lax.fori_loop(0, steps, update, 0)

    def finish(at, carry):
        out_copy(at).wait()
        return carry

    lax.fori_loop(0, steps, finish, 0)


SMEM_SPEC = pl.BlockSpec(memory_space=pltpu.SMEM)
VMEM_SPEC = pl.BlockSpec(memory_space=pltpu.VMEM)
ANY_SPEC = pl.BlockSpec(memory_space=pl.ANY)


def exchange(array, move):
    bands, cuts = lax.axis_size("band"), lax.axis_size("cuts")
    pairs = []
    for b in range(bands):
        for c in range(cuts):
            to_b, to_x, to_y, to_core = move(b, *place(c))
            if 0 <= to_b < bands:
                pairs.append((b * cuts + c, to_b * cuts + position(to_x, to_y, to_core)))
    return lax.ppermute(array, ("band", "cuts"), pairs)


def on_device(
    var_feat,
    con_feat,
    slot_column_block,
    slot_constraint_block,
    block_count,
    incidence_coefficients,
    con_first,
    con_bias,
    con_second,
    con_third,
    con_gain,
    con_shift,
    var_first,
    var_bias,
    var_second,
    var_third,
    var_gain,
    var_shift,
):
    width = var_feat.shape[1]
    slots, order = incidence_coefficients.shape[:2]
    blocks = var_feat.shape[0] // order
    groups = slots // GROUP
    columns = var_feat.reshape(blocks, order, width)
    me = lax.axis_index("cuts").astype(jnp.int32).reshape(1)
    params = pltpu.CompilerParams(vmem_limit_bytes=VMEM_BYTES)

    keep, give = pl.pallas_call(
        to_constraints_kernel,
        out_shape=(
            jax.ShapeDtypeStruct((16, order, width), F32),
            jax.ShapeDtypeStruct((16, order, width), BF16),
        ),
        in_specs=[SMEM_SPEC] * 4 + [ANY_SPEC] * 2,
        out_specs=(VMEM_SPEC, VMEM_SPEC),
        scratch_shapes=[
            pltpu.VMEM((slots, order, order), jnp.int32),
            pltpu.VMEM((blocks, order, width), BF16),
            pltpu.VMEM((33, order, width), F32),
            pltpu.SMEM((32,), jnp.int32),
            pltpu.SemaphoreType.DMA((groups,)),
            pltpu.SemaphoreType.DMA,
        ],
        compiler_params=params,
        name="to_constraints",
    )(me, block_count, slot_column_block, slot_constraint_block, incidence_coefficients, columns)

    arrived = exchange(give, lambda b, x, y, c: (b, x, y, 1 - c))
    sums = keep + arrived.astype(F32)
    mine = sums[0:4]
    for k in (2, 1, 3):
        part = sums[4 * k : 4 * k + 4].astype(BF16)
        mine = mine + exchange(part, lambda b, x, y, c, k=k: (b, x, (y + k) % 4, c)).astype(F32)
    far = exchange(mine[3].astype(BF16), lambda b, x, y, c: (b + 1, 1 - x, y, c))
    near = exchange(mine[1].astype(BF16), lambda b, x, y, c: (b + 1, x, y, c))
    side = exchange(mine[2].astype(BF16), lambda b, x, y, c: (b, 1 - x, y, c))

    con_new, turned = pl.pallas_call(
        lambda *refs: constraint_kernel(*refs[:-2], 1.0 / math.sqrt(order * slots), *refs[-2:]),
        out_shape=(
            jax.ShapeDtypeStruct((order, width), BF16),
            jax.ShapeDtypeStruct((width, order), BF16),
        ),
        name="constraints",
    )(
        mine[0],
        far,
        near,
        side,
        con_feat,
        con_first,
        con_bias.reshape(1, -1),
        con_second,
        con_third,
        con_gain.reshape(1, -1),
        con_shift.reshape(1, -1),
    )

    far = exchange(turned, lambda b, x, y, c: (b - 1, 1 - x, y, c))
    near = exchange(turned, lambda b, x, y, c: (b - 1, x, y, c))
    side = exchange(turned, lambda b, x, y, c: (b, 1 - x, y, c))
    four = jnp.stack([turned, side, near, far])
    others = {k: exchange(four, lambda b, x, y, c, k=k: (b, x, (y + k) % 4, c)) for k in (2, 1, 3)}
    sixteen = jnp.concatenate([four, others[1], others[2], others[3]], axis=0)
    rest = exchange(sixteen, lambda b, x, y, c: (b, x, y, 1 - c))
    pieces = (sixteen, rest)

    tile = 4
    var_new = pl.pallas_call(
        functools.partial(to_columns_kernel, len(pieces), 1.0 / math.sqrt(4 * order), tile),
        out_shape=jax.ShapeDtypeStruct((blocks, order, width), BF16),
        in_specs=[SMEM_SPEC] * 4 + [ANY_SPEC] * 2 + [VMEM_SPEC] * (len(pieces) + 6),
        out_specs=ANY_SPEC,
        scratch_shapes=[
            pltpu.VMEM((slots, order, order), jnp.int32),
            pltpu.VMEM((blocks, order, width), BF16),
            pltpu.VMEM((32, width, order), BF16),
            pltpu.VMEM((blocks + 1, width, order), F32),
            pltpu.VMEM((blocks, order, width), BF16),
            pltpu.SMEM((32,), jnp.int32),
            pltpu.SemaphoreType.DMA((groups,)),
            pltpu.SemaphoreType.DMA,
            pltpu.SemaphoreType.DMA((blocks // tile,)),
        ],
        compiler_params=params,
        name="to_columns",
    )(
        me,
        block_count,
        slot_column_block,
        slot_constraint_block,
        incidence_coefficients,
        columns,
        *pieces,
        var_first,
        var_bias.reshape(1, -1),
        var_second,
        var_third,
        var_gain.reshape(1, -1),
        var_shift.reshape(1, -1),
    )
    return (con_new, var_new.reshape(var_feat.shape))


def solution(mesh):
    split = P(("band", "cuts"))
    in_specs = (split,) * 6 + (P(),) * 12
    return jax.shard_map(on_device, mesh=mesh, in_specs=in_specs, out_specs=(split, split), check_vma=False)
```

```python
import functools
import math

import jax
import jax.numpy as jnp
from jax import lax
from jax.experimental import pallas as pl
from jax.experimental.pallas import tpu as pltpu
from jax.sharding import PartitionSpec as P

EPS = 1e-05
F32 = jnp.float32
BF16 = jnp.bfloat16
GROUP = 16


def place(index):
    return index // 8, (index // 2) % 4, index % 2


def position(x, y, core):
    return x * 8 + y * 2 + core


def layer_norm(values, gain, offset):
    center = values - jnp.mean(values, axis=-1, keepdims=True)
    spread = jnp.mean(center * center, axis=-1, keepdims=True)
    return center * lax.rsqrt(spread + EPS) * gain + offset


def node_update(feats, scaled_agg, w_first, bias, w_second, w_third, gain, offset):
    joined = jnp.concatenate([feats, scaled_agg.astype(BF16)], axis=1)
    hidden = jnp.maximum(jnp.dot(joined, w_first, preferred_element_type=F32) + bias, 0.0).astype(BF16)
    middle = jnp.maximum(jnp.dot(hidden, w_second, preferred_element_type=F32), 0.0).astype(BF16)
    output = jnp.dot(middle, w_third, preferred_element_type=F32)
    return layer_norm(feats.astype(F32) + output, gain, offset).astype(BF16)


def clear(acc):
    def body(block, carry):
        acc[block] = jnp.zeros(acc.shape[1:], acc.dtype)
        return carry

    lax.fori_loop(0, acc.shape[0], body, 0)


def to_constraints_kernel(
    me_ref,
    count_ref,
    col_hbm,
    row_hbm,
    coef_hbm,
    feat_hbm,
    keep_ref,
    give_ref,
    half_ref,
    coef_buf,
    feat_buf,
    acc,
    table,
    col_ref,
    row_ref,
    sem,
    feat_sem,
    index_sem,
):
    count = count_ref[0]
    groups = (count + GROUP - 1) // GROUP

    def coefficients(group):
        rows = pl.ds(group * GROUP, GROUP)
        return pltpu.make_async_copy(coef_hbm.at[rows], coef_buf.at[rows], sem.at[group])

    def start(group, carry):
        coefficients(group).start()
        return carry

    col_copy = pltpu.make_async_copy(col_hbm, col_ref, index_sem.at[0])
    row_copy = pltpu.make_async_copy(row_hbm, row_ref, index_sem.at[1])
    feat_copy = pltpu.make_async_copy(feat_hbm, feat_buf, feat_sem)
    col_copy.start()
    row_copy.start()
    coefficients(0).start()
    feat_copy.start()
    lax.fori_loop(1, groups, start, 0)
    my_x, my_y, my_core = place(me_ref[0] % 16)
    for q in range(32):
        x, y, core = place(q % 16)
        table[q] = (core ^ my_core) * 16 + ((y - my_y) & 3) * 4 + (x ^ my_x) * 2 + q // 16
    clear(acc)
    col_copy.wait()
    row_copy.wait()
    feat_copy.wait()

    def step(group, carry):
        coefficients(group).wait()
        for k in range(GROUP):
            slot = group * GROUP + k
            block = jnp.where(slot < count, table[row_ref[slot]], 32)
            coef = coef_buf[slot].astype(BF16)
            half_ref[slot] = coef
            acc[block] += jnp.dot(coef, feat_buf[col_ref[slot]], preferred_element_type=F32)
        return carry

    lax.fori_loop(0, groups, step, 0)
    keep_ref[...] = acc[pl.ds(0, 16)]
    give_ref[...] = acc[pl.ds(16, 16)].astype(BF16)


def cross_kernel(kept, arrived, feat, sums, forward, back):
    total = kept[pl.ds(0, 2)] + arrived[...].astype(F32)
    sums[...] = total
    back[0] = total[0].astype(BF16)
    back[1] = feat[...]
    forward[...] = total[1].astype(BF16)


def constraint_kernel(
    scale, last, me_ref, sums, forward, back, feat, w_first, bias, w_second, w_third, gain, offset, out, out_t
):
    own = sums[0] + forward[...].astype(F32)
    following = sums[1] + back[0].astype(F32)
    new = node_update(
        jnp.concatenate([feat[...], back[1]], axis=0),
        jnp.concatenate([own, following], axis=0) * scale,
        w_first[...],
        bias[...],
        w_second[...],
        w_third[...],
        gain[...],
        offset[...],
    )
    rows = own.shape[0]
    out[...] = new[:rows]
    out_t[0] = new[:rows].astype(F32).T.astype(BF16)
    turned = new[rows:].astype(F32).T
    out_t[1] = jnp.where(me_ref[0] >= last, jnp.zeros_like(turned), turned).astype(BF16)


def to_columns_kernel(
    scale,
    parts,
    me_ref,
    count_ref,
    col_ref,
    row_ref,
    half_ref,
    feat_ref,
    near_ref,
    far_ref,
    w_first,
    bias,
    w_second,
    w_third,
    gain,
    offset,
    out_ref,
    window,
    acc,
    out_buf,
    table,
    out_sem,
):
    count = count_ref[0]
    groups = (count + GROUP - 1) // GROUP
    my_x, my_y, my_core = place(me_ref[0] % 16)
    for q in range(32):
        x, y, core = place(q % 16)
        table[q] = (core ^ my_core) * 16 + ((my_y - y) & 3) * 4 + (x ^ my_x) * 2 + q // 16
    window[pl.ds(0, 16)] = near_ref[...]
    window[pl.ds(16, 16)] = far_ref[...]
    clear(acc)
    blocks = acc.shape[0] - 1

    def step(group, carry):
        for k in range(GROUP):
            slot = group * GROUP + k
            block = jnp.where(slot < count, col_ref[slot], blocks)
            acc[block] += jnp.dot(window[table[row_ref[slot]]], half_ref[slot], preferred_element_type=F32)
        return carry

    lax.fori_loop(0, groups, step, 0)
    tile = blocks // parts
    copies = []
    for part in range(parts):
        rows = pl.ds(part * tile, tile)
        agg = jnp.concatenate(
            [(acc[part * tile + k] * scale).astype(BF16).T for k in range(tile)], axis=0
        )
        feats = feat_ref[rows].reshape(agg.shape)
        new = node_update(
            feats, agg, w_first[...], bias[...], w_second[...], w_third[...], gain[...], offset[...]
        )
        out_buf[rows] = new.reshape(tile, -1, agg.shape[1])
        copies.append(pltpu.make_async_copy(out_buf.at[rows], out_ref.at[rows], out_sem.at[part]))
        copies[-1].start()
    for copy in copies:
        copy.wait()


SMEM_SPEC = pl.BlockSpec(memory_space=pltpu.SMEM)
VMEM_SPEC = pl.BlockSpec(memory_space=pltpu.VMEM)
HBM_SPEC = pl.BlockSpec(memory_space=pltpu.HBM)


def exchange(array, move):
    bands, cuts = lax.axis_size("band"), lax.axis_size("cuts")
    pairs = []
    for b in range(bands):
        for c in range(cuts):
            to_b, to_x, to_y, to_core = move(b, *place(c))
            if 0 <= to_b < bands:
                pairs.append((b * cuts + c, to_b * cuts + position(to_x, to_y, to_core)))
    return lax.ppermute(array, ("band", "cuts"), pairs)


def in_hbm(array):
    return pltpu.with_memory_space_constraint(array, pltpu.HBM)


def small(mib):
    return pltpu.CompilerParams(vmem_limit_bytes=mib * 1024 * 1024)


def on_device(
    var_feat,
    con_feat,
    slot_column_block,
    slot_constraint_block,
    block_count,
    incidence_coefficients,
    con_first,
    con_bias,
    con_second,
    con_third,
    con_gain,
    con_shift,
    var_first,
    var_bias,
    var_second,
    var_third,
    var_gain,
    var_shift,
):
    width = var_feat.shape[1]
    slots, order = incidence_coefficients.shape[:2]
    blocks = var_feat.shape[0] // order
    groups = slots // GROUP
    columns = var_feat.reshape(blocks, order, width)
    me = lax.axis_index(("band", "cuts")).astype(jnp.int32).reshape(1)
    bands, cuts = lax.axis_size("band"), lax.axis_size("cuts")

    keep, give, half = pl.pallas_call(
        to_constraints_kernel,
        out_shape=(
            jax.ShapeDtypeStruct((16, order, width), F32),
            jax.ShapeDtypeStruct((16, order, width), BF16),
            jax.ShapeDtypeStruct((slots, order, order), BF16),
        ),
        in_specs=[SMEM_SPEC] * 2 + [HBM_SPEC] * 4,
        out_specs=(VMEM_SPEC,) * 3,
        scratch_shapes=[
            pltpu.VMEM((slots, order, order), jnp.int32),
            pltpu.VMEM((blocks, order, width), BF16),
            pltpu.VMEM((33, order, width), F32),
            pltpu.SMEM((32,), jnp.int32),
            pltpu.SMEM((slots,), jnp.int32),
            pltpu.SMEM((slots,), jnp.int32),
            pltpu.SemaphoreType.DMA((groups,)),
            pltpu.SemaphoreType.DMA,
            pltpu.SemaphoreType.DMA((2,)),
        ],
        compiler_params=small(24),
        name="to_constraints",
    )(
        me,
        block_count,
        in_hbm(slot_column_block),
        in_hbm(slot_constraint_block),
        in_hbm(incidence_coefficients),
        in_hbm(columns),
    )

    arrived = exchange(give, lambda b, x, y, c: (b, x, y, 1 - c))
    sums = keep + arrived.astype(F32)
    mine = sums[0:4]
    parts = [sums[4 * k : 4 * k + 4].astype(BF16) for k in (2, 1, 3)]
    came = [
        exchange(part, lambda b, x, y, c, k=k: (b, x, (y + k) % 4, c)) for part, k in zip(parts, (2, 1, 3))
    ]
    for part in came:
        mine = mine + part.astype(F32)
    arrived = exchange(mine[2:4].astype(BF16), lambda b, x, y, c: (b, 1 - x, y, c))
    sums, forward, back = pl.pallas_call(
        cross_kernel,
        out_shape=(
            jax.ShapeDtypeStruct((2, order, width), F32),
            jax.ShapeDtypeStruct((order, width), BF16),
            jax.ShapeDtypeStruct((2, order, width), BF16),
        ),
        in_specs=[VMEM_SPEC] * 3,
        out_specs=(VMEM_SPEC,) * 3,
        compiler_params=small(4),
        name="across_x",
    )(mine, arrived, con_feat)
    back = exchange(back, lambda b, x, y, c: (b - 1, x, y, c))
    forward = exchange(forward, lambda b, x, y, c: (b + 1, x, y, c))

    con_new, turned = pl.pallas_call(
        functools.partial(constraint_kernel, 1.0 / math.sqrt(order * slots), (bands - 1) * cuts),
        out_shape=(
            jax.ShapeDtypeStruct((order, width), BF16),
            jax.ShapeDtypeStruct((2, width, order), BF16),
        ),
        in_specs=[SMEM_SPEC] + [VMEM_SPEC] * 10,
        out_specs=(VMEM_SPEC,) * 2,
        compiler_params=small(8),
        name="constraints",
    )(
        me,
        sums,
        forward,
        back,
        con_feat,
        con_first,
        con_bias.reshape(1, -1),
        con_second,
        con_third,
        con_gain.reshape(1, -1),
        con_shift.reshape(1, -1),
    )

    side = exchange(turned, lambda b, x, y, c: (b, 1 - x, y, c))
    four = jnp.concatenate([turned, side], axis=0)
    others = {k: exchange(four, lambda b, x, y, c, k=k: (b, x, (y + k) % 4, c)) for k in (2, 1, 3)}
    near = jnp.concatenate([four, others[1], others[2], others[3]], axis=0)
    far = exchange(near, lambda b, x, y, c: (b, x, y, 1 - c))

    parts = 1
    var_new = pl.pallas_call(
        functools.partial(to_columns_kernel, 1.0 / math.sqrt(4 * order), parts),
        out_shape=jax.ShapeDtypeStruct((blocks, order, width), BF16),
        in_specs=[SMEM_SPEC] * 4 + [VMEM_SPEC] * 10,
        out_specs=HBM_SPEC,
        scratch_shapes=[
            pltpu.VMEM((32, width, order), BF16),
            pltpu.VMEM((blocks + 1, width, order), F32),
            pltpu.VMEM((blocks, order, width), BF16),
            pltpu.SMEM((32,), jnp.int32),
            pltpu.SemaphoreType.DMA((parts,)),
        ],
        compiler_params=small(32),
        name="to_columns",
    )(
        me,
        block_count,
        slot_column_block,
        slot_constraint_block,
        half,
        columns,
        near,
        far,
        var_first,
        var_bias.reshape(1, -1),
        var_second,
        var_third,
        var_gain.reshape(1, -1),
        var_shift.reshape(1, -1),
    )
    return (con_new, var_new.reshape(var_feat.shape))


def solution(mesh):
    split = P(("band", "cuts"))
    in_specs = (split,) * 6 + (P(),) * 12
    return jax.shard_map(on_device, mesh=mesh, in_specs=in_specs, out_specs=(split, split), check_vma=False)
```

```python
import functools
import math

import jax
import jax.numpy as jnp
from jax import lax
from jax.experimental import pallas as pl
from jax.experimental.pallas import tpu as pltpu
from jax.sharding import PartitionSpec as P

EPS = 1e-05
F32 = jnp.float32
BF16 = jnp.bfloat16
GROUP = 16
COLUMN_GROUP = 40


def place(index):
    return index // 8, (index // 2) % 4, index % 2


def position(x, y, core):
    return x * 8 + y * 2 + core


def layer_norm(values, gain, offset):
    center = values - jnp.mean(values, axis=-1, keepdims=True)
    spread = jnp.mean(center * center, axis=-1, keepdims=True)
    return center * lax.rsqrt(spread + EPS) * gain + offset


def node_update(feats, scaled_agg, w_first, bias, w_second, w_third, gain, offset):
    joined = jnp.concatenate([feats, scaled_agg.astype(BF16)], axis=1)
    hidden = jnp.maximum((jnp.dot(joined, w_first, preferred_element_type=F32) + bias).astype(BF16), 0)
    middle = jnp.maximum(jnp.dot(hidden, w_second, preferred_element_type=F32).astype(BF16), 0)
    output = jnp.dot(middle, w_third, preferred_element_type=F32)
    return layer_norm(feats.astype(F32) + output, gain, offset).astype(BF16)


def clear(acc):
    def body(block, carry):
        acc[block] = jnp.zeros(acc.shape[1:], acc.dtype)
        return carry

    lax.fori_loop(0, acc.shape[0], body, 0)


def to_constraints_kernel(
    me_ref,
    count_ref,
    col_hbm,
    row_hbm,
    coef_hbm,
    feat_hbm,
    keep_ref,
    give_ref,
    half_ref,
    coef_buf,
    feat_buf,
    acc,
    table,
    col_ref,
    row_ref,
    sem,
    feat_sem,
    index_sem,
):
    count = count_ref[0]
    groups = (count + GROUP - 1) // GROUP

    def coefficients(group):
        rows = pl.ds(group * GROUP, GROUP)
        return pltpu.make_async_copy(coef_hbm.at[rows], coef_buf.at[rows], sem.at[group])

    def start(group, carry):
        coefficients(group).start()
        return carry

    col_copy = pltpu.make_async_copy(col_hbm, col_ref, index_sem.at[0])
    row_copy = pltpu.make_async_copy(row_hbm, row_ref, index_sem.at[1])
    feat_copy = pltpu.make_async_copy(feat_hbm, feat_buf, feat_sem)
    col_copy.start()
    row_copy.start()
    feat_copy.start()
    lax.fori_loop(0, groups, start, 0)
    my_core = me_ref[0] % 2
    for q in range(32):
        x, y, core = place(q % 16)
        table[q] = (core ^ my_core) * 16 + (x ^ (q // 16)) * 8 + y * 2 + q // 16
    clear(acc)
    col_copy.wait()
    row_copy.wait()
    feat_copy.wait()

    def step(group, carry):
        coefficients(group).wait()
        for k in range(GROUP):
            slot = group * GROUP + k
            block = jnp.where(slot < count, table[row_ref[slot]], 32)
            coef = coef_buf[slot].astype(BF16)
            half_ref[slot] = coef
            acc[block] += jnp.dot(coef, feat_buf[col_ref[slot]], preferred_element_type=F32)
        return carry

    lax.fori_loop(0, groups, step, 0)
    keep_ref[...] = acc[pl.ds(0, 16)]
    give_ref[...] = acc[pl.ds(16, 16)].astype(BF16)


def cross_kernel(me_ref, arrived, feat, sums, even, odd):
    total = arrived[0].astype(F32)
    for chip in range(1, arrived.shape[0]):
        total = total + arrived[chip].astype(F32)
    sums[...] = total
    lower = me_ref[0] // 16 % 2 == 0
    even[0] = jnp.where(lower, total[1], total[0]).astype(BF16)
    odd[0] = jnp.where(lower, total[0], total[1]).astype(BF16)
    even[1] = feat[...]
    odd[1] = feat[...]


def constraint_kernel(
    scale, last, me_ref, sums, odd, even, feat, w_first, bias, w_second, w_third, gain, offset, out, out_t
):
    lower = me_ref[0] // 16 % 2 == 0
    first, second = even[0].astype(F32), odd[0].astype(F32)
    next_feat = jnp.where(lower, even[1], odd[1])
    own = sums[0] + jnp.where(lower, second, first)
    following = sums[1] + jnp.where(lower, first, second)
    new = node_update(
        jnp.concatenate([feat[...], next_feat], axis=0),
        jnp.concatenate([own, following], axis=0) * scale,
        w_first[...],
        bias[...],
        w_second[...],
        w_third[...],
        gain[...],
        offset[...],
    )
    rows = own.shape[0]
    out[...] = new[:rows]
    out_t[0] = new[:rows].astype(F32).T.astype(BF16)
    turned = new[rows:].astype(F32).T
    out_t[1] = jnp.where(me_ref[0] >= last, jnp.zeros_like(turned), turned).astype(BF16)


def to_columns_kernel(
    scale,
    parts,
    me_ref,
    count_ref,
    col_ref,
    row_ref,
    half_ref,
    feat_ref,
    near_ref,
    far_ref,
    w_first,
    bias,
    w_second,
    w_third,
    gain,
    offset,
    out_ref,
    window,
    acc,
    out_buf,
    table,
    out_sem,
):
    count = count_ref[0]
    my_x, my_y, my_core = place(me_ref[0] % 16)
    for q in range(32):
        x, y, core = place(q % 16)
        table[q] = (core ^ my_core) * 16 + ((my_y - y) & 3) * 4 + (x ^ my_x ^ (q // 16)) * 2 + q // 16
    window[pl.ds(0, 16)] = near_ref[...]
    window[pl.ds(16, 16)] = far_ref[...]
    clear(acc)
    blocks = acc.shape[0] - 1

    def step(group, carry):
        for k in range(COLUMN_GROUP):
            slot = group * COLUMN_GROUP + k
            block = jnp.where(slot < count, col_ref[slot], blocks)
            acc[block] += jnp.dot(window[table[row_ref[slot]]], half_ref[slot], preferred_element_type=F32)
        return carry

    lax.fori_loop(0, (count + COLUMN_GROUP - 1) // COLUMN_GROUP, step, 0)
    tile = blocks // parts
    copies = []
    for part in range(parts):
        rows = pl.ds(part * tile, tile)
        agg = jnp.concatenate(
            [(acc[part * tile + k] * scale).astype(BF16).T for k in range(tile)], axis=0
        )
        feats = feat_ref[rows].reshape(agg.shape)
        new = node_update(
            feats, agg, w_first[...], bias[...], w_second[...], w_third[...], gain[...], offset[...]
        )
        out_buf[rows] = new.reshape(tile, -1, agg.shape[1])
        copies.append(pltpu.make_async_copy(out_buf.at[rows], out_ref.at[rows], out_sem.at[part]))
        copies[-1].start()
    for copy in copies:
        copy.wait()


SMEM_SPEC = pl.BlockSpec(memory_space=pltpu.SMEM)
VMEM_SPEC = pl.BlockSpec(memory_space=pltpu.VMEM)
HBM_SPEC = pl.BlockSpec(memory_space=pltpu.HBM)


def exchange(array, move):
    bands, cuts = lax.axis_size("band"), lax.axis_size("cuts")
    pairs = []
    for b in range(bands):
        for c in range(cuts):
            to_b, to_x, to_y, to_core = move(b, *place(c))
            if 0 <= to_b < bands:
                pairs.append((b * cuts + c, to_b * cuts + position(to_x, to_y, to_core)))
    return lax.ppermute(array, ("band", "cuts"), pairs)


def in_hbm(array):
    return pltpu.with_memory_space_constraint(array, pltpu.HBM)


def small(mib):
    return pltpu.CompilerParams(vmem_limit_bytes=mib * 1024 * 1024)


def on_device(
    var_feat,
    con_feat,
    slot_column_block,
    slot_constraint_block,
    block_count,
    incidence_coefficients,
    con_first,
    con_bias,
    con_second,
    con_third,
    con_gain,
    con_shift,
    var_first,
    var_bias,
    var_second,
    var_third,
    var_gain,
    var_shift,
):
    width = var_feat.shape[1]
    slots, order = incidence_coefficients.shape[:2]
    blocks = var_feat.shape[0] // order
    groups = slots // GROUP
    columns = var_feat.reshape(blocks, order, width)
    me = lax.axis_index(("band", "cuts")).astype(jnp.int32).reshape(1)
    bands, cuts = lax.axis_size("band"), lax.axis_size("cuts")

    keep, give, half = pl.pallas_call(
        to_constraints_kernel,
        out_shape=(
            jax.ShapeDtypeStruct((16, order, width), F32),
            jax.ShapeDtypeStruct((16, order, width), BF16),
            jax.ShapeDtypeStruct((slots, order, order), BF16),
        ),
        in_specs=[SMEM_SPEC] * 2 + [HBM_SPEC] * 4,
        out_specs=(VMEM_SPEC,) * 3,
        scratch_shapes=[
            pltpu.VMEM((slots, order, order), jnp.int32),
            pltpu.VMEM((blocks, order, width), BF16),
            pltpu.VMEM((33, order, width), F32),
            pltpu.SMEM((32,), jnp.int32),
            pltpu.SMEM((slots,), jnp.int32),
            pltpu.SMEM((slots,), jnp.int32),
            pltpu.SemaphoreType.DMA((groups,)),
            pltpu.SemaphoreType.DMA,
            pltpu.SemaphoreType.DMA((2,)),
        ],
        compiler_params=small(24),
        name="to_constraints",
    )(
        me,
        block_count,
        in_hbm(slot_column_block),
        in_hbm(slot_constraint_block),
        in_hbm(incidence_coefficients),
        in_hbm(columns),
    )

    arrived = exchange(give, lambda b, x, y, c: (b, x, y, 1 - c))
    sums = (keep + arrived.astype(F32)).astype(BF16).reshape(8, 2, order, width)
    same_core = [[position(x, y, core) for x in range(2) for y in range(4)] for core in range(2)]
    arrived = lax.all_to_all(sums, "cuts", 0, 0, tiled=True, axis_index_groups=same_core)
    sums, even, odd = pl.pallas_call(
        cross_kernel,
        out_shape=(
            jax.ShapeDtypeStruct((2, order, width), F32),
            jax.ShapeDtypeStruct((2, order, width), BF16),
            jax.ShapeDtypeStruct((2, order, width), BF16),
        ),
        in_specs=[SMEM_SPEC] + [VMEM_SPEC] * 2,
        out_specs=(VMEM_SPEC,) * 3,
        compiler_params=small(8),
        name="across_x",
    )(me, arrived, con_feat)
    odd = exchange(odd, lambda b, x, y, c: (((b + 1) ^ 1) - 1, 1 - x, y, c))
    even = exchange(even, lambda b, x, y, c: (b ^ 1, 1 - x, y, c))

    con_new, turned = pl.pallas_call(
        functools.partial(constraint_kernel, 1.0 / math.sqrt(order * slots), (bands - 1) * cuts),
        out_shape=(
            jax.ShapeDtypeStruct((order, width), BF16),
            jax.ShapeDtypeStruct((2, width, order), BF16),
        ),
        in_specs=[SMEM_SPEC] + [VMEM_SPEC] * 10,
        out_specs=(VMEM_SPEC,) * 2,
        compiler_params=small(8),
        name="constraints",
    )(
        me,
        sums,
        odd,
        even,
        con_feat,
        con_first,
        con_bias.reshape(1, -1),
        con_second,
        con_third,
        con_gain.reshape(1, -1),
        con_shift.reshape(1, -1),
    )

    side = exchange(turned, lambda b, x, y, c: (b, 1 - x, y, c))
    four = jnp.concatenate([turned, side], axis=0)
    others = {k: exchange(four, lambda b, x, y, c, k=k: (b, x, (y + k) % 4, c)) for k in (2, 1, 3)}
    near = jnp.concatenate([four, others[1], others[2], others[3]], axis=0)
    far = exchange(near, lambda b, x, y, c: (b, x, y, 1 - c))

    parts = 4
    var_new = pl.pallas_call(
        functools.partial(to_columns_kernel, 1.0 / math.sqrt(4 * order), parts),
        out_shape=jax.ShapeDtypeStruct((blocks, order, width), BF16),
        in_specs=[SMEM_SPEC] * 4 + [VMEM_SPEC] * 10,
        out_specs=HBM_SPEC,
        scratch_shapes=[
            pltpu.VMEM((32, width, order), BF16),
            pltpu.VMEM((blocks + 1, width, order), F32),
            pltpu.VMEM((blocks, order, width), BF16),
            pltpu.SMEM((32,), jnp.int32),
            pltpu.SemaphoreType.DMA((parts,)),
        ],
        compiler_params=small(32),
        name="to_columns",
    )(
        me,
        block_count,
        slot_column_block,
        slot_constraint_block,
        half,
        columns,
        near,
        far,
        var_first,
        var_bias.reshape(1, -1),
        var_second,
        var_third,
        var_gain.reshape(1, -1),
        var_shift.reshape(1, -1),
    )
    return (con_new, var_new.reshape(var_feat.shape))


def solution(mesh):
    split = P(("band", "cuts"))
    in_specs = (split,) * 6 + (P(),) * 12
    return jax.shard_map(on_device, mesh=mesh, in_specs=in_specs, out_specs=(split, split), check_vma=False)
```

```python
import functools
import math

import jax
import jax.numpy as jnp
from jax import lax
from jax.experimental import pallas as pl
from jax.experimental.pallas import tpu as pltpu
from jax.sharding import PartitionSpec as P

EPS = 1e-05
F32 = jnp.float32
BF16 = jnp.bfloat16
GROUP = 16
COLUMN_GROUP = 40


def place(index):
    return index // 8, (index // 2) % 4, index % 2


def position(x, y, core):
    return x * 8 + y * 2 + core


def layer_norm(values, gain, offset):
    center = values - jnp.mean(values, axis=-1, keepdims=True)
    spread = jnp.mean(center * center, axis=-1, keepdims=True)
    return center * lax.rsqrt(spread + EPS) * gain + offset


def node_update(feats, scaled_agg, w_first, bias, w_second, w_third, gain, offset):
    joined = jnp.concatenate([feats, scaled_agg.astype(BF16)], axis=1)
    hidden = jnp.maximum((jnp.dot(joined, w_first, preferred_element_type=F32) + bias).astype(BF16), 0)
    middle = jnp.maximum(jnp.dot(hidden, w_second, preferred_element_type=F32).astype(BF16), 0)
    output = jnp.dot(middle, w_third, preferred_element_type=F32)
    return layer_norm(feats.astype(F32) + output, gain, offset).astype(BF16)


def clear(acc):
    def body(block, carry):
        acc[block] = jnp.zeros(acc.shape[1:], acc.dtype)
        return carry

    lax.fori_loop(0, acc.shape[0], body, 0)


def to_constraints_kernel(
    me_ref,
    count_ref,
    col_hbm,
    row_hbm,
    coef_hbm,
    feat_hbm,
    keep_ref,
    give_ref,
    half_ref,
    coef_buf,
    feat_buf,
    acc,
    table,
    col_ref,
    row_ref,
    sem,
    feat_sem,
    index_sem,
):
    count = count_ref[0]
    groups = (count + GROUP - 1) // GROUP

    def coefficients(group):
        rows = pl.ds(group * GROUP, GROUP)
        return pltpu.make_async_copy(coef_hbm.at[rows], coef_buf.at[rows], sem.at[group])

    def start(group, carry):
        coefficients(group).start()
        return carry

    col_copy = pltpu.make_async_copy(col_hbm, col_ref, index_sem.at[0])
    row_copy = pltpu.make_async_copy(row_hbm, row_ref, index_sem.at[1])
    feat_copy = pltpu.make_async_copy(feat_hbm, feat_buf, feat_sem)
    col_copy.start()
    row_copy.start()
    feat_copy.start()
    lax.fori_loop(0, groups, start, 0)
    my_core = me_ref[0] % 2
    for q in range(32):
        x, y, core = place(q % 16)
        table[q] = (core ^ my_core) * 16 + (x ^ (q // 16)) * 8 + y * 2 + q // 16
    clear(acc)
    col_copy.wait()
    row_copy.wait()
    feat_copy.wait()

    def step(group, carry):
        coefficients(group).wait()
        for k in range(GROUP):
            slot = group * GROUP + k
            block = jnp.where(slot < count, table[row_ref[slot]], 32)
            coef = coef_buf[slot].astype(BF16)
            half_ref[slot] = coef
            acc[block] += jnp.dot(coef, feat_buf[col_ref[slot]], preferred_element_type=F32)
        return carry

    lax.fori_loop(0, groups, step, 0)
    keep_ref[...] = acc[pl.ds(0, 16)]
    give_ref[...] = acc[pl.ds(16, 16)].astype(BF16)


def cross_kernel(me_ref, arrived, feat, sums, even, odd):
    total = arrived[0].astype(F32)
    for chip in range(1, arrived.shape[0]):
        total = total + arrived[chip].astype(F32)
    sums[...] = total
    lower = me_ref[0] // 16 % 2 == 0
    even[0] = jnp.where(lower, total[1], total[0]).astype(BF16)
    odd[0] = jnp.where(lower, total[0], total[1]).astype(BF16)
    even[1] = feat[...]
    odd[1] = feat[...]


def constraint_kernel(
    scale, last, me_ref, sums, odd, even, feat, w_first, bias, w_second, w_third, gain, offset, out, out_t
):
    lower = me_ref[0] // 16 % 2 == 0
    first, second = even[0].astype(F32), odd[0].astype(F32)
    next_feat = jnp.where(lower, even[1], odd[1])
    own = sums[0] + jnp.where(lower, second, first)
    following = sums[1] + jnp.where(lower, first, second)
    new = node_update(
        jnp.concatenate([feat[...], next_feat], axis=0),
        jnp.concatenate([own, following], axis=0) * scale,
        w_first[...],
        bias[...],
        w_second[...],
        w_third[...],
        gain[...],
        offset[...],
    )
    rows = own.shape[0]
    out[...] = new[:rows]
    out_t[0] = new[:rows].astype(F32).T.astype(BF16)
    turned = new[rows:].astype(F32).T
    out_t[1] = jnp.where(me_ref[0] >= last, jnp.zeros_like(turned), turned).astype(BF16)


def to_columns_kernel(
    scale,
    parts,
    me_ref,
    count_ref,
    col_ref,
    row_ref,
    half_ref,
    feat_ref,
    near_ref,
    far_ref,
    w_first,
    bias,
    w_second,
    w_third,
    gain,
    offset,
    out_ref,
    window,
    acc,
    out_buf,
    table,
    out_sem,
):
    count = count_ref[0]
    my_x, my_y, my_core = place(me_ref[0] % 16)
    for q in range(32):
        x, y, core = place(q % 16)
        back = (my_y - y) & 3
        place_y = (back & 1) * 2 + back // 2
        table[q] = (core ^ my_core) * 16 + place_y * 4 + (x ^ my_x ^ (q // 16)) * 2 + q // 16
    window[pl.ds(0, 16)] = near_ref[...]
    window[pl.ds(16, 16)] = far_ref[...]
    clear(acc)
    blocks = acc.shape[0] - 1

    def step(group, carry):
        for k in range(COLUMN_GROUP):
            slot = group * COLUMN_GROUP + k
            block = jnp.where(slot < count, col_ref[slot], blocks)
            acc[block] += jnp.dot(window[table[row_ref[slot]]], half_ref[slot], preferred_element_type=F32)
        return carry

    lax.fori_loop(0, (count + COLUMN_GROUP - 1) // COLUMN_GROUP, step, 0)
    tile = blocks // parts
    copies = []
    for part in range(parts):
        rows = pl.ds(part * tile, tile)
        agg = jnp.concatenate(
            [(acc[part * tile + k] * scale).astype(BF16).T for k in range(tile)], axis=0
        )
        feats = feat_ref[rows].reshape(agg.shape)
        new = node_update(
            feats, agg, w_first[...], bias[...], w_second[...], w_third[...], gain[...], offset[...]
        )
        out_buf[rows] = new.reshape(tile, -1, agg.shape[1])
        copies.append(pltpu.make_async_copy(out_buf.at[rows], out_ref.at[rows], out_sem.at[part]))
        copies[-1].start()
    for copy in copies:
        copy.wait()


SMEM_SPEC = pl.BlockSpec(memory_space=pltpu.SMEM)
VMEM_SPEC = pl.BlockSpec(memory_space=pltpu.VMEM)
HBM_SPEC = pl.BlockSpec(memory_space=pltpu.HBM)


def exchange(array, move):
    bands, cuts = lax.axis_size("band"), lax.axis_size("cuts")
    pairs = []
    for b in range(bands):
        for c in range(cuts):
            to_b, to_x, to_y, to_core = move(b, *place(c))
            if 0 <= to_b < bands:
                pairs.append((b * cuts + c, to_b * cuts + position(to_x, to_y, to_core)))
    return lax.ppermute(array, ("band", "cuts"), pairs)


def in_hbm(array):
    return pltpu.with_memory_space_constraint(array, pltpu.HBM)


def small(mib):
    return pltpu.CompilerParams(vmem_limit_bytes=mib * 1024 * 1024)


def on_device(
    var_feat,
    con_feat,
    slot_column_block,
    slot_constraint_block,
    block_count,
    incidence_coefficients,
    con_first,
    con_bias,
    con_second,
    con_third,
    con_gain,
    con_shift,
    var_first,
    var_bias,
    var_second,
    var_third,
    var_gain,
    var_shift,
):
    width = var_feat.shape[1]
    slots, order = incidence_coefficients.shape[:2]
    blocks = var_feat.shape[0] // order
    groups = slots // GROUP
    columns = var_feat.reshape(blocks, order, width)
    me = lax.axis_index(("band", "cuts")).astype(jnp.int32).reshape(1)
    bands, cuts = lax.axis_size("band"), lax.axis_size("cuts")

    keep, give, half = pl.pallas_call(
        to_constraints_kernel,
        out_shape=(
            jax.ShapeDtypeStruct((16, order, width), F32),
            jax.ShapeDtypeStruct((16, order, width), BF16),
            jax.ShapeDtypeStruct((slots, order, order), BF16),
        ),
        in_specs=[SMEM_SPEC] * 2 + [HBM_SPEC] * 4,
        out_specs=(VMEM_SPEC,) * 3,
        scratch_shapes=[
            pltpu.VMEM((slots, order, order), jnp.int32),
            pltpu.VMEM((blocks, order, width), BF16),
            pltpu.VMEM((33, order, width), F32),
            pltpu.SMEM((32,), jnp.int32),
            pltpu.SMEM((slots,), jnp.int32),
            pltpu.SMEM((slots,), jnp.int32),
            pltpu.SemaphoreType.DMA((groups,)),
            pltpu.SemaphoreType.DMA,
            pltpu.SemaphoreType.DMA((2,)),
        ],
        compiler_params=small(24),
        name="to_constraints",
    )(
        me,
        block_count,
        in_hbm(slot_column_block),
        in_hbm(slot_constraint_block),
        in_hbm(incidence_coefficients),
        in_hbm(columns),
    )

    arrived = exchange(give, lambda b, x, y, c: (b, x, y, 1 - c))
    sums = (keep + arrived.astype(F32)).astype(BF16).reshape(8, 2, order, width)
    same_core = [[position(x, y, core) for x in range(2) for y in range(4)] for core in range(2)]
    arrived = lax.all_to_all(sums, "cuts", 0, 0, tiled=True, axis_index_groups=same_core)
    sums, even, odd = pl.pallas_call(
        cross_kernel,
        out_shape=(
            jax.ShapeDtypeStruct((2, order, width), F32),
            jax.ShapeDtypeStruct((2, order, width), BF16),
            jax.ShapeDtypeStruct((2, order, width), BF16),
        ),
        in_specs=[SMEM_SPEC] + [VMEM_SPEC] * 2,
        out_specs=(VMEM_SPEC,) * 3,
        compiler_params=small(8),
        name="across_x",
    )(me, arrived, con_feat)
    odd = exchange(odd, lambda b, x, y, c: (((b + 1) ^ 1) - 1, 1 - x, y, c))
    even = exchange(even, lambda b, x, y, c: (b ^ 1, 1 - x, y, c))

    con_new, turned = pl.pallas_call(
        functools.partial(constraint_kernel, 1.0 / math.sqrt(order * slots), (bands - 1) * cuts),
        out_shape=(
            jax.ShapeDtypeStruct((order, width), BF16),
            jax.ShapeDtypeStruct((2, width, order), BF16),
        ),
        in_specs=[SMEM_SPEC] + [VMEM_SPEC] * 10,
        out_specs=(VMEM_SPEC,) * 2,
        compiler_params=small(8),
        name="constraints",
    )(
        me,
        sums,
        odd,
        even,
        con_feat,
        con_first,
        con_bias.reshape(1, -1),
        con_second,
        con_third,
        con_gain.reshape(1, -1),
        con_shift.reshape(1, -1),
    )

    side = exchange(turned, lambda b, x, y, c: (b, 1 - x, y, c))
    four = jnp.concatenate([turned, side], axis=0)
    others = {k: exchange(four, lambda b, x, y, c, k=k: (b, x, (y + k) % 4, c)) for k in (2, 1, 3)}
    near = jnp.concatenate([four, others[2], others[1], others[3]], axis=0)
    far = exchange(near, lambda b, x, y, c: (b, x, y, 1 - c))

    parts = 4
    var_new = pl.pallas_call(
        functools.partial(to_columns_kernel, 1.0 / math.sqrt(4 * order), parts),
        out_shape=jax.ShapeDtypeStruct((blocks, order, width), BF16),
        in_specs=[SMEM_SPEC] * 4 + [VMEM_SPEC] * 10,
        out_specs=HBM_SPEC,
        scratch_shapes=[
            pltpu.VMEM((32, width, order), BF16),
            pltpu.VMEM((blocks + 1, width, order), F32),
            pltpu.VMEM((blocks, order, width), BF16),
            pltpu.SMEM((32,), jnp.int32),
            pltpu.SemaphoreType.DMA((parts,)),
        ],
        compiler_params=small(32),
        name="to_columns",
    )(
        me,
        block_count,
        slot_column_block,
        slot_constraint_block,
        half,
        columns,
        near,
        far,
        var_first,
        var_bias.reshape(1, -1),
        var_second,
        var_third,
        var_gain.reshape(1, -1),
        var_shift.reshape(1, -1),
    )
    return (con_new, var_new.reshape(var_feat.shape))


def solution(mesh):
    split = P(("band", "cuts"))
    in_specs = (split,) * 6 + (P(),) * 12
    return jax.shard_map(on_device, mesh=mesh, in_specs=in_specs, out_specs=(split, split), check_vma=False)
```

```python
import functools
import math

import jax
import jax.numpy as jnp
from jax import lax
from jax.experimental import pallas as pl
from jax.experimental.pallas import tpu as pltpu
from jax.sharding import PartitionSpec as P

EPS = 1e-05
F32 = jnp.float32
BF16 = jnp.bfloat16
GROUP = 16
COLUMN_GROUP = 40


def place(index):
    return index // 8, (index // 2) % 4, index % 2


def position(x, y, core):
    return x * 8 + y * 2 + core


def layer_norm(values, gain, offset):
    center = values - jnp.mean(values, axis=-1, keepdims=True)
    spread = jnp.mean(center * center, axis=-1, keepdims=True)
    return center * lax.rsqrt(spread + EPS) * gain + offset


def node_update(feats, scaled_agg, w_first, bias, w_second, w_third, gain, offset):
    joined = jnp.concatenate([feats, scaled_agg.astype(BF16)], axis=1)
    hidden = jnp.maximum((jnp.dot(joined, w_first, preferred_element_type=F32) + bias).astype(BF16), 0)
    middle = jnp.maximum(jnp.dot(hidden, w_second, preferred_element_type=F32).astype(BF16), 0)
    output = jnp.dot(middle, w_third, preferred_element_type=F32)
    return layer_norm(feats.astype(F32) + output, gain, offset).astype(BF16)


def clear(acc):
    def body(block, carry):
        acc[block] = jnp.zeros(acc.shape[1:], acc.dtype)
        return carry

    lax.fori_loop(0, acc.shape[0], body, 0)


def to_constraints_kernel(
    me_ref,
    count_ref,
    col_hbm,
    row_hbm,
    coef_hbm,
    feat_hbm,
    keep_ref,
    give_ref,
    half_ref,
    coef_buf,
    feat_buf,
    acc,
    table,
    col_ref,
    row_ref,
    sem,
    feat_sem,
    index_sem,
):
    count = count_ref[0]
    groups = (count + GROUP - 1) // GROUP

    def coefficients(group):
        rows = pl.ds(group * GROUP, GROUP)
        return pltpu.make_async_copy(coef_hbm.at[rows], coef_buf.at[rows], sem.at[group])

    def start(group, carry):
        coefficients(group).start()
        return carry

    col_copy = pltpu.make_async_copy(col_hbm, col_ref, index_sem.at[0])
    row_copy = pltpu.make_async_copy(row_hbm, row_ref, index_sem.at[1])
    feat_copy = pltpu.make_async_copy(feat_hbm, feat_buf, feat_sem)
    col_copy.start()
    row_copy.start()
    feat_copy.start()
    lax.fori_loop(0, groups, start, 0)
    my_core = me_ref[0] % 2
    for q in range(32):
        x, y, core = place(q % 16)
        table[q] = (core ^ my_core) * 16 + (x ^ (q // 16)) * 8 + y * 2 + q // 16
    clear(acc)
    col_copy.wait()
    row_copy.wait()
    feat_copy.wait()

    def step(group, carry):
        coefficients(group).wait()
        for k in range(GROUP):
            slot = group * GROUP + k
            block = jnp.where(slot < count, table[row_ref[slot]], 32)
            coef = coef_buf[slot].astype(BF16)
            half_ref[slot] = coef
            acc[block] += jnp.dot(coef, feat_buf[col_ref[slot]], preferred_element_type=F32)
        return carry

    lax.fori_loop(0, groups, step, 0)
    keep_ref[...] = acc[pl.ds(0, 16)]
    give_ref[...] = acc[pl.ds(16, 16)].astype(BF16)


def cross_kernel(me_ref, arrived, feat, sums, even, odd):
    total = arrived[0].astype(F32)
    for chip in range(1, arrived.shape[0]):
        total = total + arrived[chip].astype(F32)
    sums[...] = total
    lower = me_ref[0] // 16 % 2 == 0
    even[0] = jnp.where(lower, total[1], total[0]).astype(BF16)
    odd[0] = jnp.where(lower, total[0], total[1]).astype(BF16)
    even[1] = feat[...]
    odd[1] = feat[...]


def constraint_kernel(
    scale, last, me_ref, sums, odd, even, feat, w_first, bias, w_second, w_third, gain, offset, out, out_t
):
    lower = me_ref[0] // 16 % 2 == 0
    first, second = even[0].astype(F32), odd[0].astype(F32)
    next_feat = jnp.where(lower, even[1], odd[1])
    arriving = jnp.where(lower, second, first)
    own = sums[0] + jnp.where(me_ref[0] < 16, jnp.zeros_like(arriving), arriving)
    following = sums[1] + jnp.where(lower, first, second)
    new = node_update(
        jnp.concatenate([feat[...], next_feat], axis=0),
        jnp.concatenate([own, following], axis=0) * scale,
        w_first[...],
        bias[...],
        w_second[...],
        w_third[...],
        gain[...],
        offset[...],
    )
    rows = own.shape[0]
    out[...] = new[:rows]
    out_t[0] = new[:rows].T
    turned = new[rows:].T
    out_t[1] = jnp.where(me_ref[0] >= last, jnp.zeros_like(turned), turned)


def to_columns_kernel(
    scale,
    parts,
    me_ref,
    count_ref,
    col_ref,
    row_ref,
    half_ref,
    feat_ref,
    near_ref,
    far_ref,
    w_first,
    bias,
    w_second,
    w_third,
    gain,
    offset,
    out_ref,
    window,
    acc,
    out_buf,
    table,
    out_sem,
):
    count = count_ref[0]
    my_x, my_y, my_core = place(me_ref[0] % 16)
    for q in range(32):
        x, y, core = place(q % 16)
        back = (my_y - y) & 3
        place_y = (back & 1) * 2 + back // 2
        table[q] = (core ^ my_core) * 16 + place_y * 4 + (x ^ my_x ^ (q // 16)) * 2 + q // 16
    window[pl.ds(0, 16)] = near_ref[...]
    window[pl.ds(16, 16)] = far_ref[...]
    clear(acc)
    blocks = acc.shape[0] - 1

    def step(group, carry):
        for k in range(COLUMN_GROUP):
            slot = group * COLUMN_GROUP + k
            block = jnp.where(slot < count, col_ref[slot], blocks)
            acc[block] += jnp.dot(window[table[row_ref[slot]]], half_ref[slot], preferred_element_type=F32)
        return carry

    lax.fori_loop(0, (count + COLUMN_GROUP - 1) // COLUMN_GROUP, step, 0)
    tile = blocks // parts
    copies = []
    for part in range(parts):
        rows = pl.ds(part * tile, tile)
        agg = jnp.concatenate(
            [(acc[part * tile + k] * scale).astype(BF16).T for k in range(tile)], axis=0
        )
        feats = feat_ref[rows].reshape(agg.shape)
        new = node_update(
            feats, agg, w_first[...], bias[...], w_second[...], w_third[...], gain[...], offset[...]
        )
        out_buf[rows] = new.reshape(tile, -1, agg.shape[1])
        copies.append(pltpu.make_async_copy(out_buf.at[rows], out_ref.at[rows], out_sem.at[part]))
        copies[-1].start()
    for copy in copies:
        copy.wait()


SMEM_SPEC = pl.BlockSpec(memory_space=pltpu.SMEM)
VMEM_SPEC = pl.BlockSpec(memory_space=pltpu.VMEM)
HBM_SPEC = pl.BlockSpec(memory_space=pltpu.HBM)


def exchange(array, move):
    bands, cuts = lax.axis_size("band"), lax.axis_size("cuts")
    pairs = []
    for b in range(bands):
        for c in range(cuts):
            to_b, to_x, to_y, to_core = move(b, *place(c))
            if 0 <= to_b < bands:
                pairs.append((b * cuts + c, to_b * cuts + position(to_x, to_y, to_core)))
    return lax.ppermute(array, ("band", "cuts"), pairs)


def in_hbm(array):
    return pltpu.with_memory_space_constraint(array, pltpu.HBM)


def small(mib):
    return pltpu.CompilerParams(vmem_limit_bytes=mib * 1024 * 1024)


def on_device(
    var_feat,
    con_feat,
    slot_column_block,
    slot_constraint_block,
    block_count,
    incidence_coefficients,
    con_first,
    con_bias,
    con_second,
    con_third,
    con_gain,
    con_shift,
    var_first,
    var_bias,
    var_second,
    var_third,
    var_gain,
    var_shift,
):
    width = var_feat.shape[1]
    slots, order = incidence_coefficients.shape[:2]
    blocks = var_feat.shape[0] // order
    groups = slots // GROUP
    columns = var_feat.reshape(blocks, order, width)
    me = lax.axis_index(("band", "cuts")).astype(jnp.int32).reshape(1)
    bands, cuts = lax.axis_size("band"), lax.axis_size("cuts")

    keep, give, half = pl.pallas_call(
        to_constraints_kernel,
        out_shape=(
            jax.ShapeDtypeStruct((16, order, width), F32),
            jax.ShapeDtypeStruct((16, order, width), BF16),
            jax.ShapeDtypeStruct((slots, order, order), BF16),
        ),
        in_specs=[SMEM_SPEC] * 2 + [HBM_SPEC] * 4,
        out_specs=(VMEM_SPEC,) * 3,
        scratch_shapes=[
            pltpu.VMEM((slots, order, order), jnp.int32),
            pltpu.VMEM((blocks, order, width), BF16),
            pltpu.VMEM((33, order, width), F32),
            pltpu.SMEM((32,), jnp.int32),
            pltpu.SMEM((slots,), jnp.int32),
            pltpu.SMEM((slots,), jnp.int32),
            pltpu.SemaphoreType.DMA((groups,)),
            pltpu.SemaphoreType.DMA,
            pltpu.SemaphoreType.DMA((2,)),
        ],
        compiler_params=small(24),
        name="to_constraints",
    )(
        me,
        block_count,
        in_hbm(slot_column_block),
        in_hbm(slot_constraint_block),
        in_hbm(incidence_coefficients),
        in_hbm(columns),
    )

    arrived = exchange(give, lambda b, x, y, c: (b, x, y, 1 - c))
    sums = (keep + arrived.astype(F32)).astype(BF16).reshape(8, 2, order, width)
    same_core = [[position(x, y, core) for x in range(2) for y in range(4)] for core in range(2)]
    arrived = lax.all_to_all(sums, "cuts", 0, 0, tiled=True, axis_index_groups=same_core)
    sums, even, odd = pl.pallas_call(
        cross_kernel,
        out_shape=(
            jax.ShapeDtypeStruct((2, order, width), F32),
            jax.ShapeDtypeStruct((2, order, width), BF16),
            jax.ShapeDtypeStruct((2, order, width), BF16),
        ),
        in_specs=[SMEM_SPEC] + [VMEM_SPEC] * 2,
        out_specs=(VMEM_SPEC,) * 3,
        compiler_params=small(8),
        name="across_x",
    )(me, arrived, con_feat)
    def odd_partner(b, x, y, c):
        return (b, x, y, 1 - c) if b in (0, bands - 1) else (((b + 1) ^ 1) - 1, 1 - x, y, c)

    odd = exchange(odd, odd_partner)
    even = exchange(even, lambda b, x, y, c: (b ^ 1, 1 - x, y, c))

    con_new, turned = pl.pallas_call(
        functools.partial(constraint_kernel, 1.0 / math.sqrt(order * slots), (bands - 1) * cuts),
        out_shape=(
            jax.ShapeDtypeStruct((order, width), BF16),
            jax.ShapeDtypeStruct((2, width, order), BF16),
        ),
        in_specs=[SMEM_SPEC] + [VMEM_SPEC] * 10,
        out_specs=(VMEM_SPEC,) * 2,
        compiler_params=small(8),
        name="constraints",
    )(
        me,
        sums,
        odd,
        even,
        con_feat,
        con_first,
        con_bias.reshape(1, -1),
        con_second,
        con_third,
        con_gain.reshape(1, -1),
        con_shift.reshape(1, -1),
    )

    side = exchange(turned, lambda b, x, y, c: (b, 1 - x, y, c))
    four = jnp.concatenate([turned, side], axis=0)
    others = {k: exchange(four, lambda b, x, y, c, k=k: (b, x, (y + k) % 4, c)) for k in (2, 1, 3)}
    near = jnp.concatenate([four, others[2], others[1], others[3]], axis=0)
    far = exchange(near, lambda b, x, y, c: (b, x, y, 1 - c))

    parts = 4
    var_new = pl.pallas_call(
        functools.partial(to_columns_kernel, 1.0 / math.sqrt(4 * order), parts),
        out_shape=jax.ShapeDtypeStruct((blocks, order, width), BF16),
        in_specs=[SMEM_SPEC] * 4 + [VMEM_SPEC] * 10,
        out_specs=HBM_SPEC,
        scratch_shapes=[
            pltpu.VMEM((32, width, order), BF16),
            pltpu.VMEM((blocks + 1, width, order), F32),
            pltpu.VMEM((blocks, order, width), BF16),
            pltpu.SMEM((32,), jnp.int32),
            pltpu.SemaphoreType.DMA((parts,)),
        ],
        compiler_params=small(32),
        name="to_columns",
    )(
        me,
        block_count,
        slot_column_block,
        slot_constraint_block,
        half,
        columns,
        near,
        far,
        var_first,
        var_bias.reshape(1, -1),
        var_second,
        var_third,
        var_gain.reshape(1, -1),
        var_shift.reshape(1, -1),
    )
    return (con_new, var_new.reshape(var_feat.shape))


def solution(mesh):
    split = P(("band", "cuts"))
    in_specs = (split,) * 6 + (P(),) * 12
    return jax.shard_map(on_device, mesh=mesh, in_specs=in_specs, out_specs=(split, split), check_vma=False)
```

```python
import functools
import math

import jax
import jax.numpy as jnp
from jax import lax
from jax.experimental import pallas as pl
from jax.experimental.pallas import tpu as pltpu
from jax.sharding import PartitionSpec as P

EPS = 1e-05
F32 = jnp.float32
BF16 = jnp.bfloat16
GROUP = 16
COLUMN_GROUP = 40


def place(index):
    return index // 8, (index // 2) % 4, index % 2


def position(x, y, core):
    return x * 8 + y * 2 + core


def layer_norm(values, gain, offset):
    center = values - jnp.mean(values, axis=-1, keepdims=True)
    spread = jnp.mean(center * center, axis=-1, keepdims=True)
    return center * lax.rsqrt(spread + EPS) * gain + offset


def node_update(feats, scaled_agg, w_first, bias, w_second, w_third, gain, offset):
    joined = jnp.concatenate([feats, scaled_agg.astype(BF16)], axis=1)
    hidden = jnp.maximum((jnp.dot(joined, w_first, preferred_element_type=F32) + bias).astype(BF16), 0)
    middle = jnp.maximum(jnp.dot(hidden, w_second, preferred_element_type=F32).astype(BF16), 0)
    output = jnp.dot(middle, w_third, preferred_element_type=F32)
    return layer_norm(feats.astype(F32) + output, gain, offset).astype(BF16)


def clear(acc):
    def body(block, carry):
        acc[block] = jnp.zeros(acc.shape[1:], acc.dtype)
        return carry

    lax.fori_loop(0, acc.shape[0], body, 0)


def to_constraints_kernel(
    me_ref,
    count_ref,
    col_hbm,
    row_hbm,
    coef_hbm,
    feat_hbm,
    keep_ref,
    give_ref,
    half_ref,
    coef_buf,
    feat_buf,
    acc,
    table,
    col_ref,
    row_ref,
    sem,
    feat_sem,
    index_sem,
):
    count = count_ref[0]
    groups = (count + GROUP - 1) // GROUP

    def coefficients(group):
        rows = pl.ds(group * GROUP, GROUP)
        return pltpu.make_async_copy(coef_hbm.at[rows], coef_buf.at[rows], sem.at[group])

    def start(group, carry):
        coefficients(group).start()
        return carry

    col_copy = pltpu.make_async_copy(col_hbm, col_ref, index_sem.at[0])
    row_copy = pltpu.make_async_copy(row_hbm, row_ref, index_sem.at[1])
    feat_copy = pltpu.make_async_copy(feat_hbm, feat_buf, feat_sem)
    col_copy.start()
    row_copy.start()
    feat_copy.start()
    lax.fori_loop(0, groups, start, 0)
    my_core = me_ref[0] % 2
    for q in range(32):
        x, y, core = place(q % 16)
        table[q] = (core ^ my_core) * 16 + (x ^ (q // 16)) * 8 + y * 2 + q // 16
    clear(acc)
    col_copy.wait()
    row_copy.wait()
    feat_copy.wait()

    def step(group, carry):
        coefficients(group).wait()
        for k in range(GROUP):
            slot = group * GROUP + k
            block = jnp.where(slot < count, table[row_ref[slot]], 32)
            coef = coef_buf[slot].astype(BF16)
            half_ref[slot] = coef
            acc[block] += jnp.dot(coef, feat_buf[col_ref[slot]], preferred_element_type=F32)
        return carry

    lax.fori_loop(0, groups, step, 0)
    keep_ref[...] = acc[pl.ds(0, 16)]
    give_ref[...] = acc[pl.ds(16, 16)].astype(BF16)


def cross_kernel(me_ref, arrived, feat, sums, even, odd):
    total = arrived[0].astype(F32)
    for chip in range(1, arrived.shape[0]):
        total = total + arrived[chip].astype(F32)
    sums[...] = total
    lower = me_ref[0] // 16 % 2 == 0
    even[0] = jnp.where(lower, total[1], total[0]).astype(BF16)
    odd[0] = jnp.where(lower, total[0], total[1]).astype(BF16)
    even[1] = feat[...]
    odd[1] = feat[...]


def constraint_kernel(
    scale, last, me_ref, sums, odd, even, feat, w_first, bias, w_second, w_third, gain, offset, out, out_t
):
    lower = me_ref[0] // 16 % 2 == 0
    first, second = even[0].astype(F32), odd[0].astype(F32)
    next_feat = jnp.where(lower, even[1], odd[1])
    arriving = jnp.where(lower, second, first)
    own = sums[0] + jnp.where(me_ref[0] < 16, jnp.zeros_like(arriving), arriving)
    following = sums[1] + jnp.where(lower, first, second)
    new = node_update(
        jnp.concatenate([feat[...], next_feat], axis=0),
        jnp.concatenate([own, following], axis=0) * scale,
        w_first[...],
        bias[...],
        w_second[...],
        w_third[...],
        gain[...],
        offset[...],
    )
    rows = own.shape[0]
    out[...] = new[:rows]
    out_t[0] = new[:rows].T
    turned = new[rows:].T
    out_t[1] = jnp.where(me_ref[0] >= last, jnp.zeros_like(turned), turned)


def to_columns_kernel(
    scale,
    parts,
    me_ref,
    count_ref,
    col_ref,
    row_ref,
    half_ref,
    feat_ref,
    near_ref,
    far_ref,
    w_first,
    bias,
    w_second,
    w_third,
    gain,
    offset,
    out_ref,
    window,
    acc,
    out_buf,
    table,
    out_sem,
):
    count = count_ref[0]
    my_x, my_y, my_core = place(me_ref[0] % 16)
    for q in range(32):
        x, y, core = place(q % 16)
        back = (my_y - y) & 3
        place_y = jnp.where(back == 0, 0, (back + 1) % 3 + 1)
        table[q] = (core ^ my_core) * 16 + place_y * 4 + (x ^ my_x ^ (q // 16)) * 2 + q // 16
    window[pl.ds(0, 16)] = near_ref[...]
    window[pl.ds(16, 16)] = far_ref[...]
    clear(acc)
    blocks = acc.shape[0] - 1

    def step(group, carry):
        for k in range(COLUMN_GROUP):
            slot = group * COLUMN_GROUP + k
            block = jnp.where(slot < count, col_ref[slot], blocks)
            acc[block] += jnp.dot(window[table[row_ref[slot]]], half_ref[slot], preferred_element_type=F32)
        return carry

    lax.fori_loop(0, (count + COLUMN_GROUP - 1) // COLUMN_GROUP, step, 0)
    tile = blocks // parts
    copies = []
    for part in range(parts):
        rows = pl.ds(part * tile, tile)
        agg = jnp.concatenate(
            [(acc[part * tile + k] * scale).astype(BF16).T for k in range(tile)], axis=0
        )
        feats = feat_ref[rows].reshape(agg.shape)
        new = node_update(
            feats, agg, w_first[...], bias[...], w_second[...], w_third[...], gain[...], offset[...]
        )
        out_buf[rows] = new.reshape(tile, -1, agg.shape[1])
        copies.append(pltpu.make_async_copy(out_buf.at[rows], out_ref.at[rows], out_sem.at[part]))
        copies[-1].start()
    for copy in copies:
        copy.wait()


SMEM_SPEC = pl.BlockSpec(memory_space=pltpu.SMEM)
VMEM_SPEC = pl.BlockSpec(memory_space=pltpu.VMEM)
HBM_SPEC = pl.BlockSpec(memory_space=pltpu.HBM)


def exchange(array, move):
    bands, cuts = lax.axis_size("band"), lax.axis_size("cuts")
    pairs = []
    for b in range(bands):
        for c in range(cuts):
            to_b, to_x, to_y, to_core = move(b, *place(c))
            if 0 <= to_b < bands:
                pairs.append((b * cuts + c, to_b * cuts + position(to_x, to_y, to_core)))
    return lax.ppermute(array, ("band", "cuts"), pairs)


def in_hbm(array):
    return pltpu.with_memory_space_constraint(array, pltpu.HBM)


def small(mib):
    return pltpu.CompilerParams(vmem_limit_bytes=mib * 1024 * 1024)


def on_device(
    var_feat,
    con_feat,
    slot_column_block,
    slot_constraint_block,
    block_count,
    incidence_coefficients,
    con_first,
    con_bias,
    con_second,
    con_third,
    con_gain,
    con_shift,
    var_first,
    var_bias,
    var_second,
    var_third,
    var_gain,
    var_shift,
):
    width = var_feat.shape[1]
    slots, order = incidence_coefficients.shape[:2]
    blocks = var_feat.shape[0] // order
    groups = slots // GROUP
    columns = var_feat.reshape(blocks, order, width)
    me = lax.axis_index(("band", "cuts")).astype(jnp.int32).reshape(1)
    bands, cuts = lax.axis_size("band"), lax.axis_size("cuts")

    keep, give, half = pl.pallas_call(
        to_constraints_kernel,
        out_shape=(
            jax.ShapeDtypeStruct((16, order, width), F32),
            jax.ShapeDtypeStruct((16, order, width), BF16),
            jax.ShapeDtypeStruct((slots, order, order), BF16),
        ),
        in_specs=[SMEM_SPEC] * 2 + [HBM_SPEC] * 4,
        out_specs=(VMEM_SPEC,) * 3,
        scratch_shapes=[
            pltpu.VMEM((slots, order, order), jnp.int32),
            pltpu.VMEM((blocks, order, width), BF16),
            pltpu.VMEM((33, order, width), F32),
            pltpu.SMEM((32,), jnp.int32),
            pltpu.SMEM((slots,), jnp.int32),
            pltpu.SMEM((slots,), jnp.int32),
            pltpu.SemaphoreType.DMA((groups,)),
            pltpu.SemaphoreType.DMA,
            pltpu.SemaphoreType.DMA((2,)),
        ],
        compiler_params=small(24),
        name="to_constraints",
    )(
        me,
        block_count,
        in_hbm(slot_column_block),
        in_hbm(slot_constraint_block),
        in_hbm(incidence_coefficients),
        in_hbm(columns),
    )

    arrived = exchange(give, lambda b, x, y, c: (b, x, y, 1 - c))
    sums = (keep + arrived.astype(F32)).astype(BF16).reshape(8, 2, order, width)
    same_core = [[position(x, y, core) for x in range(2) for y in range(4)] for core in range(2)]
    arrived = lax.all_to_all(sums, "cuts", 0, 0, tiled=True, axis_index_groups=same_core)
    sums, even, odd = pl.pallas_call(
        cross_kernel,
        out_shape=(
            jax.ShapeDtypeStruct((2, order, width), F32),
            jax.ShapeDtypeStruct((2, order, width), BF16),
            jax.ShapeDtypeStruct((2, order, width), BF16),
        ),
        in_specs=[SMEM_SPEC] + [VMEM_SPEC] * 2,
        out_specs=(VMEM_SPEC,) * 3,
        compiler_params=small(8),
        name="across_x",
    )(me, arrived, con_feat)
    def odd_partner(b, x, y, c):
        return (b, x, y, 1 - c) if b in (0, bands - 1) else (((b + 1) ^ 1) - 1, 1 - x, y, c)

    odd = exchange(odd, odd_partner)
    even = exchange(even, lambda b, x, y, c: (b ^ 1, 1 - x, y, c))

    con_new, turned = pl.pallas_call(
        functools.partial(constraint_kernel, 1.0 / math.sqrt(order * slots), (bands - 1) * cuts),
        out_shape=(
            jax.ShapeDtypeStruct((order, width), BF16),
            jax.ShapeDtypeStruct((2, width, order), BF16),
        ),
        in_specs=[SMEM_SPEC] + [VMEM_SPEC] * 10,
        out_specs=(VMEM_SPEC,) * 2,
        compiler_params=small(8),
        name="constraints",
    )(
        me,
        sums,
        odd,
        even,
        con_feat,
        con_first,
        con_bias.reshape(1, -1),
        con_second,
        con_third,
        con_gain.reshape(1, -1),
        con_shift.reshape(1, -1),
    )

    side = exchange(turned, lambda b, x, y, c: (b, 1 - x, y, c))
    four = jnp.concatenate([turned, side], axis=0)
    others = {k: exchange(four, lambda b, x, y, c, k=k: (b, x, (y + k) % 4, c)) for k in (2, 1, 3)}
    near = jnp.concatenate([four, others[2], others[3], others[1]], axis=0)
    far = exchange(near, lambda b, x, y, c: (b, x, y, 1 - c))

    parts = 4
    var_new = pl.pallas_call(
        functools.partial(to_columns_kernel, 1.0 / math.sqrt(4 * order), parts),
        out_shape=jax.ShapeDtypeStruct((blocks, order, width), BF16),
        in_specs=[SMEM_SPEC] * 4 + [VMEM_SPEC] * 10,
        out_specs=HBM_SPEC,
        scratch_shapes=[
            pltpu.VMEM((32, width, order), BF16),
            pltpu.VMEM((blocks + 1, width, order), F32),
            pltpu.VMEM((blocks, order, width), BF16),
            pltpu.SMEM((32,), jnp.int32),
            pltpu.SemaphoreType.DMA((parts,)),
        ],
        compiler_params=small(32),
        name="to_columns",
    )(
        me,
        block_count,
        slot_column_block,
        slot_constraint_block,
        half,
        columns,
        near,
        far,
        var_first,
        var_bias.reshape(1, -1),
        var_second,
        var_third,
        var_gain.reshape(1, -1),
        var_shift.reshape(1, -1),
    )
    return (con_new, var_new.reshape(var_feat.shape))


def solution(mesh):
    split = P(("band", "cuts"))
    in_specs = (split,) * 6 + (P(),) * 12
    return jax.shard_map(on_device, mesh=mesh, in_specs=in_specs, out_specs=(split, split), check_vma=False)
```
